128 devices in a mesh: gx: 8 (over z, core), gy: 16 (over x, y).
Axes of the slice: x: 4, y: 4, z: 4, core: 2. Of those that a mesh axis runs over, the one named last changes fastest.
Arguments:
- compressed: bfloat16 [128, 1536], P(None, 'gx'), may hold values from -6 to 6
- query_up: bfloat16 [1536, 24576], P('gx', 'gy'), may hold values from -0.15625 to 0.15625
- key_absorb: bfloat16 [128, 128, 512], P('gy'), may hold values from -1 to 1
- value_up: bfloat16 [128, 512, 128], P('gy'), may hold values from -0.25 to 0.25
- out_proj: bfloat16 [16384, 7168], P('gy', 'gx'), may hold values from -0.046875 to 0.046875
- cache_latent: bfloat16 [128, 16384, 512], P(('gx', 'gy')), may hold values from -6 to 6
- cache_rope: bfloat16 [128, 64, 16384], P(('gx', 'gy')), may hold values from -6 to 6
- lengths: int32 [128], replicated, may hold values from 1 to 16384, as said below
- holder: int32 [128], replicated, may hold values from 0 to 127, each once
Outputs:
- attended: bfloat16 [128, 7168], P('gy', 'gx')
The draws below stay inside these ranges and needn't reach their ends.
Inputs may be any that keep to these rules, and one draw needn't show every extreme that they name: `lengths`: some request has exactly 16384 valid positions.
All inputs are finite; a program needn't handle non-finite values.
Results may differ from the reference program's by a relative error of at most 0.02.
Values may be sent and summed in bfloat16 or wider, within the bound.
No kernel may reach another device: no remote copies, remote signals or barrier semaphores. Data moves between devices by JAX's collectives and lax.ppermute only.
A program may use at most 128 MiB of HBM per device.

```python
import math
import jax
import jax.numpy as jnp
from jax import lax

D = 7168
H = 128
QL = 1536
KVL = 512
ROPE = 64
NOPE = 128
VH = 128
LMAX = 16384
B = 128


def draw_lengths(key, part):
    key = jax.random.fold_in(key, 7)
    first_key, second_key = jax.random.split(key)
    drawn = jax.random.randint(first_key, (B,), 1, LMAX + 1)
    chosen = jax.random.randint(second_key, (), 0, B)
    return jnp.where(jnp.arange(B) == chosen, LMAX, drawn).astype(jnp.int32)


def draw_key_absorb(key, part):
    key = jax.random.fold_in(key, 11)
    first_key = jax.random.fold_in(key, 0)
    entries = jnp.clip(jax.random.normal(first_key, (H, NOPE, KVL), jnp.float32), -6.0, 6.0) / math.sqrt(NOPE)
    return jnp.clip(entries, -1.0, 1.0).astype(jnp.bfloat16)


def draw_cache_latent(key, part):
    key = jax.random.fold_in(key, 13)
    first_key = jax.random.fold_in(key, 0)
    latent = jnp.clip(jax.random.normal(first_key, (B, LMAX, KVL), jnp.float32), -6.0, 6.0)
    return latent.astype(jnp.bfloat16)


def levels(stream_key, dims, cuts, least, high):
    def one(dim, blocks):
        draws = jax.random.uniform(jax.random.fold_in(jax.random.fold_in(stream_key, 6), dim), (blocks,), jnp.float32, least / len(cuts), high / len(cuts))
        return jnp.repeat(jnp.exp(draws), dims[dim] // blocks).reshape((-1,) + (1,) * (len(dims) - dim - 1))

    level = one(*cuts[0])
    for cut in cuts[1:]:
        level = level * one(*cut)
    return level


def noise(own_key, shape, scale, limit, cuts=(), held_as=jnp.bfloat16):
    factor_of = levels(own_key, shape, cuts, -0.22, 0.18) if cuts else 1.0
    result = jax.random.normal(own_key, shape, jnp.float32) * scale * factor_of
    return jnp.minimum(jnp.maximum(result, -limit), limit).astype(held_as)


def setup_inputs(seed: int = 0) -> dict:
    arg_keys = jax.random.split(jax.random.key(seed), 10)
    compressed = noise(arg_keys[0], (B, QL), 1.0, 6.0, ((1, 8),))
    query_up = noise(arg_keys[1], (QL, H * (NOPE + ROPE)), QL ** -0.5, 0.15625, ((0, 8), (1, 16)))
    key_absorb = draw_key_absorb(jax.random.fold_in(arg_keys[9], 71), 0)
    value_up = noise(arg_keys[3], (H, KVL, VH), KVL ** -0.5, 0.25, ((0, 16),))
    out_proj = noise(arg_keys[4], (H * VH, D), (H * VH) ** -0.5, 0.046875, ((0, 16), (1, 8)))
    cache_latent = draw_cache_latent(jax.random.fold_in(arg_keys[9], 71), 0)
    cache_rope = noise(arg_keys[6], (B, ROPE, LMAX), 1.0, 6.0, ((0, 128),))
    lengths = draw_lengths(jax.random.fold_in(arg_keys[9], 71), 0)
    holder = jax.random.permutation(arg_keys[8], B).astype(jnp.int32)
    return {"compressed": compressed, "query_up": query_up, "key_absorb": key_absorb, "value_up": value_up, "out_proj": out_proj, "cache_latent": cache_latent, "cache_rope": cache_rope, "lengths": lengths, "holder": holder}


def rotate(halves, positions):
    half_width = halves.shape[-1] // 2
    frequency = 10000.0 ** (-2.0 * jnp.arange(half_width).astype(jnp.float32) / halves.shape[-1])
    angles = positions.astype(jnp.float32)[:, None, None] * frequency
    former = halves[..., :half_width]
    latter = halves[..., half_width:]
    return jnp.concatenate([former * jnp.cos(angles) - latter * jnp.sin(angles), former * jnp.sin(angles) + latter * jnp.cos(angles)], axis=-1)

def attend(query_lat, query_rope, latent, rope_keys, length):
    scores = lax.dot_general(query_lat, latent, (((1,), (1,)), ((), ())), preferred_element_type=jnp.float32)
    scores = scores + jnp.dot(query_rope, rope_keys, preferred_element_type=jnp.float32)
    scores = scores * (1.0 / math.sqrt(NOPE + ROPE))
    places = jnp.arange(latent.shape[0]).astype(jnp.int32)
    scores = jnp.where(places[None, :] < length, scores, -1e+30)
    largest = lax.optimization_barrier(jnp.max(scores, axis=1, keepdims=True))
    expos = jnp.exp(scores - largest)
    weights = (expos / lax.optimization_barrier(jnp.sum(expos, axis=1, keepdims=True))).astype(jnp.bfloat16)
    return jnp.dot(weights, latent, preferred_element_type=jnp.float32).astype(jnp.bfloat16)

def reference(compressed, query_up, key_absorb, value_up, out_proj, cache_latent, cache_rope, lengths, holder):
    batch = compressed.shape[0]
    projected = jnp.dot(compressed, query_up, preferred_element_type=jnp.float32).reshape(batch, H, NOPE + ROPE)
    nope_part = projected[..., :NOPE].astype(jnp.bfloat16)
    rope_part = rotate(projected[..., NOPE:], lengths - 1).astype(jnp.bfloat16)
    absorbed = jnp.einsum('bhn,hnc->bhc', nope_part.astype(jnp.float32), key_absorb.astype(jnp.float32)).astype(jnp.bfloat16)

    def one_slot(pieces):
        request, latent, rope_keys = pieces
        return attend(absorbed[request], rope_part[request], latent, rope_keys, lengths[request])
    by_slot = lax.map(one_slot, (holder, cache_latent, cache_rope))
    by_request = jnp.zeros_like(by_slot).at[holder].set(by_slot)
    head_values = jnp.einsum('bhc,hcv->bhv', by_request.astype(jnp.float32), value_up.astype(jnp.float32)).astype(jnp.bfloat16)
    head_values = head_values.reshape(batch, H * VH)
    return jnp.dot(head_values, out_proj, preferred_element_type=jnp.float32).astype(jnp.bfloat16)
```

```python
import math

import jax
import jax.numpy as jnp
from jax import lax
from jax.experimental import pallas as pl
from jax.experimental.pallas import tpu as pltpu
from jax.sharding import PartitionSpec as P

KVL = 512
ROPE = 64
NOPE = 128
HEAD = NOPE + ROPE
VH = 128
WIDE = 640
CHUNK = 4096
PIECE = 2048
VMEM = pl.BlockSpec(memory_space=pltpu.VMEM)
SMEM = pl.BlockSpec(memory_space=pltpu.SMEM)
ANY = pl.BlockSpec(memory_space=pl.ANY)
F32 = jnp.float32
BF16 = jnp.bfloat16


def dot(a, b, contract_a=1, contract_b=0):
    return lax.dot_general(
        a, b, (((contract_a,), (contract_b,)), ((), ())), preferred_element_type=F32
    )


def holder_matrix(holder_row):
    count = holder_row.shape[1]
    requests = lax.broadcasted_iota(jnp.int32, (count, count), 0)
    return (requests == holder_row).astype(F32).astype(BF16)


def project_kernel(holder_ref, compressed_ref, query_up_ref, mine_ref, other_ref, part_ref):
    core = lax.rem(lax.axis_index("gx"), 2)
    by_slot = dot(compressed_ref[...], holder_matrix(holder_ref[...])).astype(BF16)
    part_ref[...] = dot(by_slot, query_up_ref[...], 0, 0)
    for z in range(4):
        mine_ref[z * 16 : z * 16 + 16, :] = part_ref[pl.ds(z * 32 + core * 16, 16), :]
        other_ref[z * 16 : z * 16 + 16, :] = part_ref[pl.ds(z * 32 + 16 - core * 16, 16), :].astype(
            BF16
        )


def pair_kernel(mine_ref, got_ref, own_ref, one_ref, two_ref, three_ref):
    z = lax.div(lax.axis_index("gx"), 2)
    for k, out_ref in enumerate((own_ref, one_ref, two_ref, three_ref)):
        rows = pl.ds(pl.multiple_of((z ^ k) * 16, 16), 16)
        out_ref[...] = (mine_ref[rows, :] + got_ref[rows, :].astype(F32)).astype(out_ref.dtype)


def absorb_kernel(
    own_ref, one_ref, two_ref, three_ref, keep_ref, minus_ref, plus_ref, absorb_ref, out_ref, wide_ref
):
    queries = (
        own_ref[...]
        + one_ref[...].astype(F32)
        + two_ref[...].astype(F32)
        + three_ref[...].astype(F32)
    )
    width = queries.shape[1]
    half = ROPE // 2
    queries = (
        queries * keep_ref[...]
        + pltpu.roll(queries, width - half, 1) * minus_ref[...]
        + pltpu.roll(queries, half, 1) * plus_ref[...]
    )
    shifted = pltpu.roll(queries, width - 64, 1)
    blank = jnp.zeros((queries.shape[0], WIDE - KVL - ROPE), F32)
    for h in range(absorb_ref.shape[0]):
        start = h * HEAD
        source = queries if start % 128 == 0 else shifted
        start -= start % 128
        nope = source[:, start : start + NOPE].astype(BF16)
        start = h * HEAD + NOPE
        source = queries if start % 128 == 0 else shifted
        start -= start % 128
        rope = source[:, start : start + ROPE]
        wide_ref[:, h, :KVL] = dot(nope, absorb_ref[h])
        wide_ref[:, h, KVL:] = jnp.concatenate([rope, blank], axis=1)
    out_ref[...] = wide_ref[...].reshape(out_ref.shape).astype(BF16)


def attend_kernel(
    length_ref, query_ref, latent_hbm, rope_hbm, out_ref, latent, rope, scores, top, total, acc, sems
):
    length = length_ref[0]
    places = latent.shape[0]
    scale = math.log2(math.e) / math.sqrt(HEAD)

    def copies(i):
        at = pl.ds(i * PIECE, PIECE)
        return (
            pltpu.make_async_copy(latent_hbm.at[0, at, :], latent.at[at, :], sems.at[0, i]),
            pltpu.make_async_copy(rope_hbm.at[0, :, at], rope.at[:, at], sems.at[1, i]),
        )

    for i in range(places // PIECE):

        @pl.when(i * PIECE < length)
        def _():
            for copy in copies(i):
                copy.start()

    top[...] = jnp.full(top.shape, -1e30, F32)
    total[...] = jnp.zeros(total.shape, F32)
    acc[...] = jnp.zeros(acc.shape, F32)
    query_lat = query_ref[:, :KVL]
    query_rope = query_ref[:, KVL : KVL + ROPE]
    per = CHUNK // PIECE
    for c in range(places // CHUNK):
        at = pl.ds(c * CHUNK, CHUNK)

        @pl.when(c * CHUNK < length)
        def _():
            for i in range(c * per, c * per + per):

                @pl.when(i * PIECE < length)
                def _():
                    for copy in copies(i):
                        copy.wait()

                @pl.when(i * PIECE >= length)
                def _():
                    latent[pl.ds(i * PIECE, PIECE), :] = jnp.zeros((PIECE, KVL), BF16)

            s = dot(latent[at, :], query_lat, 1, 1) + dot(rope[:, at], query_rope, 0, 1)
            position = c * CHUNK + lax.broadcasted_iota(jnp.int32, s.shape, 0)
            s = jnp.where(position < length, s, -1e30)
            scores[at, :] = s
            top[...] = jnp.maximum(top[...], jnp.max(s, axis=0, keepdims=True))

    for c in range(places // CHUNK):
        at = pl.ds(c * CHUNK, CHUNK)

        @pl.when(c * CHUNK < length)
        def _():
            p = jnp.exp2((scores[at, :] - top[...]) * scale)
            total[...] += jnp.sum(p, axis=0, keepdims=True)
            acc[...] += dot(p.astype(BF16), latent[at, :], 0, 0)

    sums = jnp.transpose(jnp.broadcast_to(total[...], (128, 128)))
    out_ref[...] = (acc[...] / sums[:, :1]).astype(BF16)


def value_kernel(latent_ref, value_up_ref, out_ref, wide_ref):
    heads = value_up_ref.shape[0]
    wide_ref[...] = latent_ref[...].astype(F32).reshape(wide_ref.shape)
    for h in range(heads):
        out_ref[:, h * VH : h * VH + VH] = dot(
            wide_ref[:, h, :].astype(BF16), value_up_ref[h]
        ).astype(BF16)


def output_kernel(holder_ref, own_ref, one_ref, two_ref, three_ref, pair_ref, proj_ref, out_ref):
    count = holder_ref.shape[1]
    gx = lax.axis_index("gx")
    core = lax.rem(gx, 2)
    z = lax.div(gx, 2)
    row = lax.broadcasted_iota(jnp.int32, (count, count), 1)
    slot = (
        (((row >> 4) & 3) ^ z) * 32
        + ((row >> 6) ^ core) * 16
        + (row & 15)
    )
    slots = lax.broadcasted_iota(jnp.int32, (count, count), 0)
    place = (slots == slot).astype(F32).astype(BF16)
    order = dot(holder_matrix(holder_ref[...]), place).astype(BF16)
    values = jnp.concatenate(
        [own_ref[...], one_ref[...], two_ref[...], three_ref[...], pair_ref[...]], axis=0
    )
    values = dot(order, values).astype(BF16)
    out_ref[...] = dot(values, proj_ref[...]).astype(BF16)


def call(kernel, out_shape, in_specs, scratch=(), limit=None, name=None):
    many = isinstance(out_shape, (list, tuple))
    return pl.pallas_call(
        kernel,
        out_shape=out_shape,
        in_specs=in_specs,
        out_specs=[VMEM] * len(out_shape) if many else VMEM,
        scratch_shapes=list(scratch),
        compiler_params=pltpu.CompilerParams(vmem_limit_bytes=limit) if limit else None,
        name=name,
    )


def swap(array, distance, axis="gx"):
    count = lax.axis_size(axis)
    return lax.ppermute(array, axis, [(i, i ^ distance) for i in range(count)])


def tables(lengths, holder, heads):
    half = ROPE // 2
    first = lax.axis_index("gx") * 16
    own = lax.dynamic_slice_in_dim(holder, first, 16, 0)
    own_lengths = jnp.sum(
        jnp.where(own[:, None] == jnp.arange(holder.shape[0])[None, :], lengths[None, :], 0), axis=1
    )
    frequency = 10000.0 ** (-2.0 * jnp.arange(half).astype(F32) / ROPE)
    angles = (own_lengths - 1).astype(F32)[:, None] * frequency
    cos, sin = jnp.cos(angles), jnp.sin(angles)
    ones = jnp.ones((16, NOPE), F32)
    none = jnp.zeros((16, NOPE), F32)
    blank = jnp.zeros((16, half), F32)
    keep = jnp.tile(jnp.concatenate([ones, cos, cos], axis=1), (1, heads))
    minus = jnp.tile(jnp.concatenate([none, -sin, blank], axis=1), (1, heads))
    plus = jnp.tile(jnp.concatenate([none, blank, sin], axis=1), (1, heads))
    return keep, minus, plus


def local(
    compressed, query_up, key_absorb, value_up, out_proj, cache_latent, cache_rope, lengths, holder
):
    shape = jax.ShapeDtypeStruct
    index_gx = lax.axis_index("gx")
    index_gy = lax.axis_index("gy")
    batch = compressed.shape[0]
    width = query_up.shape[1]
    heads = key_absorb.shape[0]
    places = cache_latent.shape[1]
    holder_row = holder.reshape(1, batch)
    slot = index_gx * 16 + index_gy
    length = jnp.sum(
        jnp.where(jnp.arange(batch) == lax.dynamic_slice_in_dim(holder, slot, 1, 0), lengths, 0)
    ).reshape(1)
    keep, minus, plus = tables(lengths, holder, heads)

    mine, other = call(
        project_kernel,
        (shape((64, width), F32), shape((64, width), BF16)),
        [VMEM] * 3,
        [pltpu.VMEM((batch, width), F32)],
        name="project",
    )(holder_row, compressed.T, query_up)
    got = swap(other, 1)
    own, one, two, three = call(
        pair_kernel,
        (shape((16, width), F32),) + (shape((16, width), BF16),) * 3,
        [VMEM] * 2,
        name="pair",
    )(mine, got)
    one, two, three = swap(one, 2), swap(two, 4), swap(three, 6)
    queries = call(
        absorb_kernel,
        shape((16 * heads, WIDE), BF16),
        [VMEM] * 8,
        [pltpu.VMEM((16, heads, WIDE), F32)],
        name="absorb",
    )(own, one, two, three, keep, minus, plus, key_absorb)
    queries = lax.all_to_all(queries, "gy", split_axis=0, concat_axis=0, tiled=True)

    latent_out = call(
        attend_kernel,
        shape((128, KVL), BF16),
        [SMEM, VMEM, ANY, ANY],
        [
            pltpu.VMEM((places, KVL), BF16),
            pltpu.VMEM((ROPE, places), BF16),
            pltpu.VMEM((places, 128), F32),
            pltpu.VMEM((1, 128), F32),
            pltpu.VMEM((1, 128), F32),
            pltpu.VMEM((128, KVL), F32),
            pltpu.SemaphoreType.DMA((2, places // PIECE)),
        ],
        limit=44 * 2**20,
        name="attend",
    )(length, queries, cache_latent, cache_rope)

    returned = lax.all_to_all(latent_out, "gy", split_axis=0, concat_axis=0, tiled=True)
    values = call(
        value_kernel,
        shape((16, heads * VH), BF16),
        [VMEM] * 2,
        [pltpu.VMEM((16, heads, KVL), F32)],
        name="values",
    )(returned, value_up)
    one, two, three = swap(values, 2), swap(values, 4), swap(values, 6)
    pair = swap(jnp.concatenate([values, one, two, three], axis=0), 1)
    partial = call(
        output_kernel,
        shape((batch, out_proj.shape[1]), BF16),
        [VMEM] * 7,
        name="output",
    )(holder_row, values, one, two, three, pair, out_proj)
    partial = lax.all_to_all(partial, "gy", split_axis=0, concat_axis=0, tiled=True)
    partial = partial.reshape(16, batch // 16, out_proj.shape[1])
    return jnp.sum(partial.astype(F32), axis=0).astype(BF16)


def solution(mesh):
    in_specs = (
        P(None, "gx"),
        P("gx", "gy"),
        P("gy", None, None),
        P("gy", None, None),
        P("gy", "gx"),
        P(("gx", "gy"), None, None),
        P(("gx", "gy"), None, None),
        P(),
        P(),
    )
    out_specs = P("gy", "gx")
    return jax.shard_map(local, mesh=mesh, in_specs=in_specs, out_specs=out_specs, check_vma=False)
```

```python
import math

import jax
import jax.numpy as jnp
import numpy as np
from jax import lax
from jax.experimental import pallas as pl
from jax.experimental.pallas import tpu as pltpu
from jax.sharding import Mesh
from jax.sharding import PartitionSpec as P

KVL = 512
ROPE = 64
NOPE = 128
HEAD = NOPE + ROPE
VH = 128
WIDE = 640
CHUNK = 4096
PARTS = 4
VMEM = pl.BlockSpec(memory_space=pltpu.VMEM)
SMEM = pl.BlockSpec(memory_space=pltpu.SMEM)
ANY = pl.BlockSpec(memory_space=pl.ANY)
F32 = jnp.float32
BF16 = jnp.bfloat16


def dot(a, b, contract_a=1, contract_b=0):
    return lax.dot_general(
        a, b, (((contract_a,), (contract_b,)), ((), ())), preferred_element_type=F32
    )


def holder_matrix(holder_row):
    count = holder_row.shape[1]
    requests = lax.broadcasted_iota(jnp.int32, (count, count), 0)
    return (requests == holder_row).astype(F32).astype(BF16)


def order_matrix(holder_row):
    count = holder_row.shape[1]
    row = lax.broadcasted_iota(jnp.int32, (count, count), 1)
    core = (row >> 6) ^ lax.axis_index("c")
    slot = ((row & 3) * 2 + core) * 16 + ((row >> 2) & 15)
    slots = lax.broadcasted_iota(jnp.int32, (count, count), 0)
    place = (slots == slot).astype(F32).astype(BF16)
    return dot(holder_matrix(holder_row), place).astype(BF16)


def project_kernel(
    holder_hbm, compressed_hbm, query_up_hbm, mine_ref, other_ref, holder, compressed, query_up, sems
):
    half, width = mine_ref.shape
    part = width // PARTS
    copies = [
        pltpu.make_async_copy(holder_hbm, holder, sems.at[0]),
        pltpu.make_async_copy(compressed_hbm, compressed, sems.at[1]),
    ]
    for i in range(PARTS):
        at = pl.ds(i * part, part)
        copies.append(
            pltpu.make_async_copy(query_up_hbm.at[:, at], query_up.at[:, at], sems.at[2 + i])
        )
    for copy in copies:
        copy.start()
    copies[0].wait()
    order = order_matrix(holder[...])
    copies[1].wait()
    by_slot = dot(compressed[...], order).astype(BF16)
    for i in range(PARTS):
        at = slice(i * part, i * part + part)
        copies[2 + i].wait()
        term = dot(by_slot, query_up[:, at], 0, 0)
        mine_ref[:, at] = term[:half]
        other_ref[:, at] = term[half:].astype(BF16)


def prepare_kernel(
    holder_ref, lengths_ref, frequency_ref, absorb_hbm, angle_ref, absorb_ref, place_ref, sem
):
    copy = pltpu.make_async_copy(absorb_hbm, absorb_ref, sem)
    copy.start()
    core = lax.axis_index("c")
    for j in range(place_ref.shape[0]):
        slot = ((j & 3) * 2 + core) * 16 + (j >> 2)
        place = (lengths_ref[holder_ref[slot]] - 1).astype(F32)
        place_ref[j : j + 1, :] = jnp.full((1, 128), place, F32)
    angles = place_ref[...] * frequency_ref[...]
    sin = jnp.sin(angles)
    lane = lax.broadcasted_iota(jnp.int32, angles.shape, 1)
    former = (lane & (ROPE - 1)) < ROPE // 2
    angle_ref[0] = jnp.cos(angles)
    angle_ref[1] = jnp.where(former, -sin, 0.0)
    angle_ref[2] = jnp.where(former, 0.0, sin)
    copy.wait()


def absorb_kernel(
    mine_ref, got_ref, angle_ref, absorb_ref, latent_hbm, rope_hbm, out_ref, wide_ref
):
    queries = mine_ref[...] + got_ref[...].astype(F32)
    lane = lax.broadcasted_iota(jnp.int32, (queries.shape[0], 128), 1)
    low = lane < 64
    for h in range(0, absorb_ref.shape[0], 2):
        start = h * HEAD
        first = queries[:, start : start + 128]
        second = queries[:, start + 128 : start + 256]
        third = queries[:, start + 256 : start + 384]
        other = pltpu.roll(jnp.where(low, third, second), 64, 1)
        rope = jnp.where(low, second, third)
        rope = (
            rope * angle_ref[0]
            + pltpu.roll(rope, 128 - ROPE // 2, 1) * angle_ref[1]
            + pltpu.roll(rope, ROPE // 2, 1) * angle_ref[2]
        )
        wide_ref[:, h, :KVL] = dot(first.astype(BF16), absorb_ref[h])
        wide_ref[:, h, KVL:] = jnp.where(low, rope, 0.0)
        wide_ref[:, h + 1, :KVL] = dot(other.astype(BF16), absorb_ref[h + 1])
        wide_ref[:, h + 1, KVL:] = jnp.where(low, 0.0, rope)
    out_ref[...] = wide_ref[...].reshape(out_ref.shape).astype(BF16)


def attend_kernel(holder_ref, lengths_ref, query_ref, latent, rope, out_ref, scores):
    slot = (lax.axis_index("z") * 2 + lax.axis_index("c")) * 16
    slot += lax.axis_index("x") * 4 + lax.axis_index("y")
    length = lengths_ref[holder_ref[slot]]
    places = latent.shape[1]
    groups, chips, heads = out_ref.shape[:3]
    count = groups * heads

    query = query_ref[:, 0].astype(F32)
    for z in range(1, chips):
        query += query_ref[:, z].astype(F32)
    query = query.reshape(count, WIDE) * (math.log2(math.e) / math.sqrt(HEAD))
    query_lat = query[:, :KVL].astype(BF16)
    query_rope = (query[:, KVL : KVL + ROPE] + query[:, KVL + ROPE :]).astype(BF16)
    tops = []
    for start in range(0, places, CHUNK):
        at = slice(start, start + CHUNK)
        s = dot(latent[0, at, :], query_lat, 1, 1) + dot(rope[0, :, at], query_rope, 0, 1)
        position = start + lax.broadcasted_iota(jnp.int32, s.shape, 0)
        s = jnp.where(position < length, s, -1e30)
        scores[at, :] = s
        tops.append(jnp.max(s, axis=0, keepdims=True))
    top = tops[0]
    for other in tops[1:]:
        top = jnp.maximum(top, other)
    total = jnp.zeros((1, count), F32)
    acc = jnp.zeros((count, KVL), F32)
    for start in range(0, places, CHUNK):
        at = slice(start, start + CHUNK)
        p = jnp.exp2(scores[at, :] - top)
        total += jnp.sum(p, axis=0, keepdims=True)
        acc += dot(p.astype(BF16), latent[0, at, :], 0, 0)
    total = jnp.transpose(jnp.broadcast_to(total, (count, count)))[:, :1]
    result = (acc / total).reshape(groups, heads, KVL).astype(BF16)
    for z in range(chips):
        out_ref[:, z] = result


def value_kernel(latent_ref, value_up_ref, out_ref, wide_ref):
    heads = value_up_ref.shape[0]
    wide_ref[...] = latent_ref[...].astype(F32).reshape(wide_ref.shape)
    for h in range(heads):
        out_ref[:, h * VH : h * VH + VH] = dot(
            wide_ref[:, h, :].astype(BF16), value_up_ref[h]
        ).astype(BF16)


def output_kernel(holder_ref, own_ref, pair_ref, proj_ref, out_ref):
    values = jnp.concatenate([own_ref[...], pair_ref[...]], axis=0)
    values = dot(order_matrix(holder_ref[...]), values).astype(BF16)
    out_ref[...] = dot(values, proj_ref[...]).astype(BF16)


def call(kernel, out_shape, in_specs, scratch=(), limit=8, name=None, cost=None):
    many = isinstance(out_shape, (list, tuple))
    return pl.pallas_call(
        kernel,
        out_shape=out_shape,
        in_specs=in_specs,
        out_specs=[VMEM] * len(out_shape) if many else VMEM,
        scratch_shapes=list(scratch),
        compiler_params=pltpu.CompilerParams(vmem_limit_bytes=limit * 2**20),
        name=name,
        cost_estimate=cost,
    )


def stay(array):
    return pltpu.with_memory_space_constraint(array, pltpu.HBM)


def keep(array):
    return pltpu.with_memory_space_constraint(array, pltpu.VMEM)


def swap_cores(array):
    return lax.ppermute(array, "c", [(0, 1), (1, 0)])


def exchange(array, axes):
    return lax.all_to_all(array, axes, split_axis=0, concat_axis=0, tiled=True)


def local(
    compressed, query_up, key_absorb, value_up, out_proj, cache_latent, cache_rope, lengths, holder
):
    shape = jax.ShapeDtypeStruct
    batch = compressed.shape[0]
    width = query_up.shape[1]
    heads = key_absorb.shape[0]
    places = cache_latent.shape[1]
    chips = lax.axis_size("z")
    groups = lax.axis_size("x") * lax.axis_size("y")
    own = chips * groups
    holder_row = holder.reshape(1, batch)
    half = np.arange(ROPE // 2, dtype=np.float32)
    frequency = (10000.0 ** (-2.0 * half / ROPE)).astype(np.float32)
    frequency = jnp.asarray(np.tile(frequency, 4)[None, :])

    mine, other = call(
        project_kernel,
        (pltpu.VMEM((own, width), F32), pltpu.VMEM((own, width), BF16)),
        [ANY] * 3,
        [
            pltpu.VMEM((1, batch), jnp.int32),
            pltpu.VMEM((compressed.shape[1], batch), BF16),
            pltpu.VMEM(query_up.shape, BF16),
            pltpu.SemaphoreType.DMA((2 + PARTS,)),
        ],
        name="project",
    )(stay(holder_row), stay(compressed.T), stay(query_up))
    got = swap_cores(other)
    angles, absorb_in = call(
        prepare_kernel,
        (pltpu.VMEM((3, own, 128), F32), pltpu.VMEM(key_absorb.shape, BF16)),
        [SMEM, SMEM, VMEM, ANY],
        [pltpu.VMEM((own, 128), F32), pltpu.SemaphoreType.DMA],
        name="prepare",
    )(stay(holder), stay(lengths), stay(frequency), stay(key_absorb))
    queries = call(
        absorb_kernel,
        shape((own * heads, WIDE), BF16),
        [VMEM] * 4 + [ANY] * 2,
        [pltpu.VMEM((own, heads, WIDE), F32)],
        name="absorb",
    )(mine, got, angles, absorb_in, stay(cache_latent), stay(cache_rope))
    queries = exchange(queries, ("x", "y", "z"))

    latent_out = call(
        attend_kernel,
        shape((groups, chips, heads, KVL), BF16),
        [SMEM, SMEM, VMEM, VMEM, VMEM],
        [pltpu.VMEM((places, 128), F32)],
        limit=20,
        name="attend",
    )(
        holder,
        lengths,
        queries.reshape(groups, chips, heads, WIDE),
        keep(cache_latent),
        keep(cache_rope),
    )

    returned = exchange(latent_out.reshape(own * heads, KVL), ("x", "y", "z"))
    values = call(
        value_kernel,
        shape((own, heads * VH), BF16),
        [VMEM] * 2,
        [pltpu.VMEM((own, heads, KVL), F32)],
        name="values",
    )(returned, value_up)
    partial = call(
        output_kernel,
        shape((batch, out_proj.shape[1]), BF16),
        [VMEM] * 4,
        name="output",
    )(holder_row, values, swap_cores(values), out_proj)
    partial = exchange(partial, ("x", "y"))
    partial = partial.reshape(groups, batch // groups, out_proj.shape[1])
    return jnp.sum(partial.astype(F32), axis=0).astype(BF16)


def solution(mesh):
    mesh = Mesh(mesh.devices.reshape(4, 2, 4, 4), ("z", "c", "x", "y"))
    gx, gy, both = ("z", "c"), ("x", "y"), ("z", "c", "x", "y")
    in_specs = (
        P(None, gx),
        P(gx, gy),
        P(gy, None, None),
        P(gy, None, None),
        P(gy, gx),
        P(both, None, None),
        P(both, None, None),
        P(),
        P(),
    )
    out_specs = P(gy, gx)
    return jax.shard_map(local, mesh=mesh, in_specs=in_specs, out_specs=out_specs, check_vma=False)
```

```python
import math

import jax
import jax.numpy as jnp
import numpy as np
from jax import lax
from jax.experimental import pallas as pl
from jax.experimental.pallas import tpu as pltpu
from jax.sharding import Mesh
from jax.sharding import PartitionSpec as P

KVL = 512
ROPE = 64
NOPE = 128
HEAD = NOPE + ROPE
VH = 128
WIDE = 640
CHUNK = 8192
PARTS = 4
VMEM = pl.BlockSpec(memory_space=pltpu.VMEM)
SMEM = pl.BlockSpec(memory_space=pltpu.SMEM)
ANY = pl.BlockSpec(memory_space=pl.ANY)
F32 = jnp.float32
BF16 = jnp.bfloat16


def dot(a, b, contract_a=1, contract_b=0):
    return lax.dot_general(
        a, b, (((contract_a,), (contract_b,)), ((), ())), preferred_element_type=F32
    )


def holder_matrix(holder_row):
    count = holder_row.shape[1]
    requests = lax.broadcasted_iota(jnp.int32, (count, count), 0)
    return (requests == holder_row).astype(F32).astype(BF16)


def place_matrix(count):
    row = lax.broadcasted_iota(jnp.int32, (count, count), 1)
    core = (row >> 6) ^ lax.axis_index("c")
    slot = ((row & 3) * 2 + core) * 16 + ((row >> 2) & 15)
    slots = lax.broadcasted_iota(jnp.int32, (count, count), 0)
    return (slots == slot).astype(F32).astype(BF16)


def order_matrix(holder_row):
    return dot(holder_matrix(holder_row), place_matrix(holder_row.shape[1])).astype(BF16)


def project_kernel(
    holder_hbm,
    lengths_hbm,
    frequency_hbm,
    compressed_hbm,
    query_up_hbm,
    absorb_hbm,
    mine_ref,
    other_ref,
    angle_ref,
    absorb_ref,
    holder,
    lengths,
    frequency,
    compressed,
    query_up,
    sems,
):
    half, width = mine_ref.shape
    part = width // PARTS
    pairs = [
        (holder_hbm, holder),
        (lengths_hbm, lengths),
        (frequency_hbm, frequency),
        (compressed_hbm, compressed),
    ]
    for i in range(PARTS):
        at = pl.ds(i * part, part)
        pairs.append((query_up_hbm.at[:, at], query_up.at[:, at]))
    pairs.append((absorb_hbm, absorb_ref))
    copies = [
        pltpu.make_async_copy(source, target, sems.at[i]) for i, (source, target) in enumerate(pairs)
    ]
    for copy in copies:
        copy.start()
    for copy in copies[:3]:
        copy.wait()
    held = holder_matrix(holder[...])
    place = place_matrix(held.shape[0])
    order = dot(held, place).astype(BF16)
    turned = dot(place, held, 0, 1)[:half]
    last = jnp.sum(turned * (lengths[...] - 1).astype(F32), axis=1, keepdims=True)
    angles = last * frequency[...]
    sin = jnp.sin(angles)
    lane = lax.broadcasted_iota(jnp.int32, angles.shape, 1)
    former = (lane & (ROPE - 1)) < ROPE // 2
    angle_ref[0] = jnp.cos(angles)
    angle_ref[1] = jnp.where(former, -sin, 0.0)
    angle_ref[2] = jnp.where(former, 0.0, sin)
    copies[3].wait()
    by_slot = dot(compressed[...], order).astype(BF16)
    for i in range(PARTS):
        at = slice(i * part, i * part + part)
        copies[4 + i].wait()
        term = dot(by_slot, query_up[:, at], 0, 0)
        mine_ref[:, at] = term[:half]
        other_ref[:, at] = term[half:].astype(BF16)
    copies[-1].wait()


def absorb_kernel(
    mine_ref, got_ref, angle_ref, absorb_ref, latent_hbm, rope_hbm, out_ref, wide_ref
):
    queries = mine_ref[...] + got_ref[...].astype(F32)
    lane = lax.broadcasted_iota(jnp.int32, (queries.shape[0], 128), 1)
    low = lane < 64
    for h in range(0, absorb_ref.shape[0], 2):
        start = h * HEAD
        first = queries[:, start : start + 128]
        second = queries[:, start + 128 : start + 256]
        third = queries[:, start + 256 : start + 384]
        other = pltpu.roll(jnp.where(low, third, second), 64, 1)
        rope = jnp.where(low, second, third)
        rope = (
            rope * angle_ref[0]
            + pltpu.roll(rope, 128 - ROPE // 2, 1) * angle_ref[1]
            + pltpu.roll(rope, ROPE // 2, 1) * angle_ref[2]
        )
        wide_ref[:, h, :KVL] = dot(first.astype(BF16), absorb_ref[h])
        wide_ref[:, h, KVL:] = jnp.where(low, rope, 0.0)
        wide_ref[:, h + 1, :KVL] = dot(other.astype(BF16), absorb_ref[h + 1])
        wide_ref[:, h + 1, KVL:] = jnp.where(low, 0.0, rope)
    out_ref[...] = wide_ref[...].reshape(out_ref.shape).astype(BF16)


def attend_kernel(holder_ref, lengths_ref, query_ref, latent, rope, out_ref, scores, acc):
    slot = (lax.axis_index("z") * 2 + lax.axis_index("c")) * 16
    slot += lax.axis_index("x") * 4 + lax.axis_index("y")
    length = lengths_ref[holder_ref[slot]]
    places = latent.shape[1]
    groups, chips, heads = out_ref.shape[:3]
    count = groups * heads

    query = query_ref[:, 0].astype(F32)
    for z in range(1, chips):
        query += query_ref[:, z].astype(F32)
    query = query.reshape(count, WIDE) * (math.log2(math.e) / math.sqrt(HEAD))
    query_lat = query[:, :KVL].astype(BF16)
    query_rope = (query[:, KVL : KVL + ROPE] + query[:, KVL + ROPE :]).astype(BF16)

    def score(i, top):
        start = pl.multiple_of(i * CHUNK, CHUNK)
        at = pl.ds(start, CHUNK)
        s = dot(latent[0, at, :], query_lat, 1, 1) + dot(rope[0, :, at], query_rope, 0, 1)
        position = start + lax.broadcasted_iota(jnp.int32, s.shape, 0)
        s = jnp.where(position < length, s, -1e30)
        scores[at, :] = s
        return jnp.maximum(top, jnp.max(s, axis=0, keepdims=True))

    top = lax.fori_loop(0, places // CHUNK, score, jnp.full((1, count), -1e30, F32))
    acc[...] = jnp.zeros(acc.shape, F32)

    def gather(i, total):
        at = pl.ds(pl.multiple_of(i * CHUNK, CHUNK), CHUNK)
        p = jnp.exp2(scores[at, :] - top)
        acc[...] += dot(p.astype(BF16), latent[0, at, :], 0, 0)
        return total + jnp.sum(p, axis=0, keepdims=True)

    total = lax.fori_loop(0, places // CHUNK, gather, jnp.zeros((1, count), F32))
    total = jnp.transpose(jnp.broadcast_to(total, (count, count)))[:, :1]
    result = (acc[...] / total).reshape(groups, heads, KVL).astype(BF16)
    for z in range(chips):
        out_ref[:, z] = result


def value_kernel(latent_ref, value_up_ref, out_ref, wide_ref):
    heads = value_up_ref.shape[0]
    wide_ref[...] = latent_ref[...].astype(F32).reshape(wide_ref.shape)
    for h in range(heads):
        out_ref[:, h * VH : h * VH + VH] = dot(
            wide_ref[:, h, :].astype(BF16), value_up_ref[h]
        ).astype(BF16)


def output_kernel(holder_ref, own_ref, pair_ref, proj_ref, out_ref):
    values = jnp.concatenate([own_ref[...], pair_ref[...]], axis=0)
    values = dot(order_matrix(holder_ref[...]), values).astype(BF16)
    out_ref[...] = dot(values, proj_ref[...]).astype(BF16)


def call(kernel, out_shape, in_specs, scratch=(), limit=8, name=None, cost=None):
    many = isinstance(out_shape, (list, tuple))
    return pl.pallas_call(
        kernel,
        out_shape=out_shape,
        in_specs=in_specs,
        out_specs=[VMEM] * len(out_shape) if many else VMEM,
        scratch_shapes=list(scratch),
        compiler_params=pltpu.CompilerParams(vmem_limit_bytes=limit * 2**20),
        name=name,
        cost_estimate=cost,
    )


def stay(array):
    return pltpu.with_memory_space_constraint(array, pltpu.HBM)


def keep(array):
    return pltpu.with_memory_space_constraint(array, pltpu.VMEM)


def swap_cores(array):
    return lax.ppermute(array, "c", [(0, 1), (1, 0)])


def exchange(array, axes):
    return lax.all_to_all(array, axes, split_axis=0, concat_axis=0, tiled=True)


def local(
    compressed, query_up, key_absorb, value_up, out_proj, cache_latent, cache_rope, lengths, holder
):
    shape = jax.ShapeDtypeStruct
    batch = compressed.shape[0]
    width = query_up.shape[1]
    heads = key_absorb.shape[0]
    places = cache_latent.shape[1]
    chips = lax.axis_size("z")
    groups = lax.axis_size("x") * lax.axis_size("y")
    own = chips * groups
    holder_row = holder.reshape(1, batch)
    half = np.arange(ROPE // 2, dtype=np.float32)
    frequency = (10000.0 ** (-2.0 * half / ROPE)).astype(np.float32)
    frequency = jnp.asarray(np.tile(frequency, 4)[None, :])

    mine, other, angles, absorb_in = call(
        project_kernel,
        (
            pltpu.VMEM((own, width), F32),
            pltpu.VMEM((own, width), BF16),
            pltpu.VMEM((3, own, 128), F32),
            pltpu.VMEM(key_absorb.shape, BF16),
        ),
        [ANY] * 6,
        [
            pltpu.VMEM((1, batch), jnp.int32),
            pltpu.VMEM((1, batch), jnp.int32),
            pltpu.VMEM((1, 128), F32),
            pltpu.VMEM((compressed.shape[1], batch), BF16),
            pltpu.VMEM(query_up.shape, BF16),
            pltpu.SemaphoreType.DMA((5 + PARTS,)),
        ],
        name="project",
    )(
        stay(holder_row),
        stay(lengths.reshape(1, batch)),
        stay(frequency),
        stay(compressed.T),
        stay(query_up),
        stay(key_absorb),
    )
    got = swap_cores(other)
    queries = call(
        absorb_kernel,
        shape((own * heads, WIDE), BF16),
        [VMEM] * 4 + [ANY] * 2,
        [pltpu.VMEM((own, heads, WIDE), F32)],
        name="absorb",
    )(mine, got, angles, absorb_in, stay(cache_latent), stay(cache_rope))
    queries = exchange(queries, ("x", "y", "z"))

    latent_out = call(
        attend_kernel,
        shape((groups, chips, heads, KVL), BF16),
        [SMEM, SMEM, VMEM, VMEM, VMEM],
        [pltpu.VMEM((places, 128), F32), pltpu.VMEM((128, KVL), F32)],
        limit=20,
        name="attend",
    )(
        holder,
        lengths,
        queries.reshape(groups, chips, heads, WIDE),
        keep(cache_latent),
        keep(cache_rope),
    )

    returned = exchange(latent_out.reshape(own * heads, KVL), ("x", "y", "z"))
    values = call(
        value_kernel,
        shape((own, heads * VH), BF16),
        [VMEM] * 2,
        [pltpu.VMEM((own, heads, KVL), F32)],
        name="values",
    )(returned, value_up)
    partial = call(
        output_kernel,
        shape((batch, out_proj.shape[1]), BF16),
        [VMEM] * 4,
        name="output",
    )(holder_row, values, swap_cores(values), out_proj)
    partial = exchange(partial, ("x", "y"))
    partial = partial.reshape(groups, batch // groups, out_proj.shape[1])
    return jnp.sum(partial.astype(F32), axis=0).astype(BF16)


def solution(mesh):
    mesh = Mesh(mesh.devices.reshape(4, 2, 4, 4), ("z", "c", "x", "y"))
    gx, gy, both = ("z", "c"), ("x", "y"), ("z", "c", "x", "y")
    in_specs = (
        P(None, gx),
        P(gx, gy),
        P(gy, None, None),
        P(gy, None, None),
        P(gy, gx),
        P(both, None, None),
        P(both, None, None),
        P(),
        P(),
    )
    out_specs = P(gy, gx)
    return jax.shard_map(local, mesh=mesh, in_specs=in_specs, out_specs=out_specs, check_vma=False)
```

```python
import math

import jax
import jax.numpy as jnp
import numpy as np
from jax import lax
from jax.experimental import pallas as pl
from jax.experimental.pallas import tpu as pltpu
from jax.sharding import Mesh
from jax.sharding import PartitionSpec as P

KVL = 512
ROPE = 64
NOPE = 128
HEAD = NOPE + ROPE
VH = 128
WIDE = 640
SCORED = 8192
GATHERED = 16384
PARTS = 1
VMEM = pl.BlockSpec(memory_space=pltpu.VMEM)
SMEM = pl.BlockSpec(memory_space=pltpu.SMEM)
ANY = pl.BlockSpec(memory_space=pl.ANY)
F32 = jnp.float32
BF16 = jnp.bfloat16


def dot(a, b, contract_a=1, contract_b=0):
    return lax.dot_general(
        a, b, (((contract_a,), (contract_b,)), ((), ())), preferred_element_type=F32
    )


def holder_matrix(holder_row):
    count = holder_row.shape[1]
    requests = lax.broadcasted_iota(jnp.int32, (count, count), 0)
    return (requests == holder_row).astype(F32).astype(BF16)


def place_matrix(count):
    row = lax.broadcasted_iota(jnp.int32, (count, count), 1)
    core = (row >> 6) ^ lax.axis_index("c")
    slot = ((row & 3) * 2 + core) * 16 + ((row >> 2) & 15)
    slots = lax.broadcasted_iota(jnp.int32, (count, count), 0)
    return (slots == slot).astype(F32).astype(BF16)


def project_kernel(
    holder_hbm,
    lengths_hbm,
    frequency_hbm,
    compressed_hbm,
    query_up_hbm,
    absorb_hbm,
    mine_ref,
    other_ref,
    angle_ref,
    order_ref,
    absorb_ref,
    holder,
    lengths,
    frequency,
    compressed,
    query_up,
    sems,
):
    half, width = mine_ref.shape
    part = width // PARTS
    pairs = [
        (holder_hbm, holder),
        (lengths_hbm, lengths),
        (frequency_hbm, frequency),
        (compressed_hbm, compressed),
    ]
    for i in range(PARTS):
        at = pl.ds(i * part, part)
        pairs.append((query_up_hbm.at[:, at], query_up.at[:, at]))
    pairs.append((absorb_hbm, absorb_ref))
    copies = [
        pltpu.make_async_copy(source, target, sems.at[i]) for i, (source, target) in enumerate(pairs)
    ]
    for copy in copies:
        copy.start()
    for copy in copies[:3]:
        copy.wait()
    held = holder_matrix(holder[...])
    place = place_matrix(held.shape[0])
    order_ref[...] = dot(held, place).astype(BF16)
    turned = dot(place, held, 0, 1)[:half]
    last = jnp.sum(turned * (lengths[...] - 1).astype(F32), axis=1, keepdims=True)
    angle_ref[...] = last * frequency[...]
    copies[3].wait()
    by_slot = dot(compressed[...], order_ref[...]).astype(BF16)
    for i in range(PARTS):
        at = slice(i * part, i * part + part)
        copies[4 + i].wait()
        term = dot(by_slot, query_up[:, at], 0, 0)
        mine_ref[:, at] = term[:half]
        other_ref[:, at] = term[half:].astype(BF16)
    copies[-1].wait()


def angle_kernel(angle_ref, out_ref):
    angles = angle_ref[...]
    sin = jnp.sin(angles)
    lane = lax.broadcasted_iota(jnp.int32, angles.shape, 1)
    former = (lane & (ROPE - 1)) < ROPE // 2
    out_ref[0] = jnp.cos(angles)
    out_ref[1] = jnp.where(former, -sin, 0.0)
    out_ref[2] = jnp.where(former, 0.0, sin)


def absorb_kernel(
    mine_ref, got_ref, angle_ref, absorb_ref, latent_hbm, rope_hbm, out_ref, wide_ref
):
    queries = mine_ref[...] + got_ref[...].astype(F32)
    lane = lax.broadcasted_iota(jnp.int32, (queries.shape[0], 128), 1)
    low = lane < 64
    for h in range(0, absorb_ref.shape[0], 2):
        start = h * HEAD
        first = queries[:, start : start + 128]
        second = queries[:, start + 128 : start + 256]
        third = queries[:, start + 256 : start + 384]
        other = pltpu.roll(jnp.where(low, third, second), 64, 1)
        rope = jnp.where(low, second, third)
        rope = (
            rope * angle_ref[0]
            + pltpu.roll(rope, 128 - ROPE // 2, 1) * angle_ref[1]
            + pltpu.roll(rope, ROPE // 2, 1) * angle_ref[2]
        )
        wide_ref[:, h, :KVL] = dot(first.astype(BF16), absorb_ref[h])
        wide_ref[:, h, KVL:] = jnp.where(low, rope, 0.0)
        wide_ref[:, h + 1, :KVL] = dot(other.astype(BF16), absorb_ref[h + 1])
        wide_ref[:, h + 1, KVL:] = jnp.where(low, 0.0, rope)
    out_ref[...] = wide_ref[...].reshape(out_ref.shape).astype(BF16)


def attend_kernel(holder_ref, lengths_ref, query_ref, latent, rope, out_ref, scores, acc):
    slot = (lax.axis_index("z") * 2 + lax.axis_index("c")) * 16
    slot += lax.axis_index("x") * 4 + lax.axis_index("y")
    length = lengths_ref[holder_ref[slot]]
    places = latent.shape[1]
    groups, chips, heads = out_ref.shape[:3]
    count = groups * heads

    query = query_ref[:, 0].astype(F32)
    for z in range(1, chips):
        query += query_ref[:, z].astype(F32)
    query = query.reshape(count, WIDE) * (math.log2(math.e) / math.sqrt(HEAD))
    query_lat = query[:, :KVL].astype(BF16)
    query_rope = (query[:, KVL : KVL + ROPE] + query[:, KVL + ROPE :]).astype(BF16)

    def score(i, top):
        start = pl.multiple_of(i * SCORED, SCORED)
        at = pl.ds(start, SCORED)
        s = dot(latent[0, at, :], query_lat, 1, 1) + dot(rope[0, :, at], query_rope, 0, 1)
        position = start + lax.broadcasted_iota(jnp.int32, s.shape, 0)
        s = jnp.where(position < length, s, -1e30)
        scores[at, :] = s
        return jnp.maximum(top, jnp.max(s, axis=0, keepdims=True))

    top = lax.fori_loop(0, places // SCORED, score, jnp.full((1, count), -1e30, F32))
    acc[...] = jnp.zeros(acc.shape, F32)

    def gather(i, total):
        at = pl.ds(pl.multiple_of(i * GATHERED, GATHERED), GATHERED)
        p = jnp.exp2(scores[at, :] - top)
        acc[...] += dot(p.astype(BF16), latent[0, at, :], 0, 0)
        return total + jnp.sum(p, axis=0, keepdims=True)

    total = lax.fori_loop(0, places // GATHERED, gather, jnp.zeros((1, count), F32))
    total = jnp.transpose(jnp.broadcast_to(total, (count, count)))[:, :1]
    result = (acc[...] / total).reshape(groups, heads, KVL).astype(BF16)
    for z in range(chips):
        out_ref[:, z] = result


def value_kernel(latent_ref, value_up_ref, out_ref):
    heads = value_up_ref.shape[0]
    rows = latent_ref.shape[0]
    slots = rows // heads
    row = lax.broadcasted_iota(jnp.int32, (rows, rows), 0)
    came = lax.broadcasted_iota(jnp.int32, (rows, rows), 1)
    by_head = ((row % slots) * heads + row // slots == came).astype(F32).astype(BF16)
    latents = dot(by_head, latent_ref[...]).astype(BF16)
    for h in range(heads):
        out_ref[:, h * VH : h * VH + VH] = dot(
            latents[h * slots : h * slots + slots], value_up_ref[h]
        ).astype(BF16)


def output_kernel(order_ref, own_ref, pair_ref, proj_ref, out_ref):
    values = jnp.concatenate([own_ref[...], pair_ref[...]], axis=0)
    values = dot(order_ref[...], values).astype(BF16)
    out_ref[...] = dot(values, proj_ref[...]).astype(BF16)


def call(kernel, out_shape, in_specs, scratch=(), limit=8, name=None, cost=None):
    many = isinstance(out_shape, (list, tuple))
    return pl.pallas_call(
        kernel,
        out_shape=out_shape,
        in_specs=in_specs,
        out_specs=[VMEM] * len(out_shape) if many else VMEM,
        scratch_shapes=list(scratch),
        compiler_params=pltpu.CompilerParams(vmem_limit_bytes=limit * 2**20),
        name=name,
        cost_estimate=cost,
    )


def stay(array):
    return pltpu.with_memory_space_constraint(array, pltpu.HBM)


def keep(array):
    return pltpu.with_memory_space_constraint(array, pltpu.VMEM)


def swap_cores(array):
    return lax.ppermute(array, "c", [(0, 1), (1, 0)])


def exchange(array, axes):
    return lax.all_to_all(array, axes, split_axis=0, concat_axis=0, tiled=True)


def local(
    compressed, query_up, key_absorb, value_up, out_proj, cache_latent, cache_rope, lengths, holder
):
    shape = jax.ShapeDtypeStruct
    batch = compressed.shape[0]
    width = query_up.shape[1]
    heads = key_absorb.shape[0]
    places = cache_latent.shape[1]
    chips = lax.axis_size("z")
    groups = lax.axis_size("x") * lax.axis_size("y")
    own = chips * groups
    holder_row = holder.reshape(1, batch)
    half = np.arange(ROPE // 2, dtype=np.float32)
    frequency = (10000.0 ** (-2.0 * half / ROPE)).astype(np.float32)
    frequency = jnp.asarray(np.tile(frequency, 4)[None, :])

    mine, other, angles, order, absorb_in = call(
        project_kernel,
        (
            pltpu.VMEM((own, width), F32),
            pltpu.VMEM((own, width), BF16),
            pltpu.VMEM((own, 128), F32),
            pltpu.VMEM((batch, batch), BF16),
            pltpu.VMEM(key_absorb.shape, BF16),
        ),
        [ANY] * 6,
        [
            pltpu.VMEM((1, batch), jnp.int32),
            pltpu.VMEM((1, batch), jnp.int32),
            pltpu.VMEM((1, 128), F32),
            pltpu.VMEM((compressed.shape[1], batch), BF16),
            pltpu.VMEM(query_up.shape, BF16),
            pltpu.SemaphoreType.DMA((5 + PARTS,)),
        ],
        name="project",
    )(
        stay(holder_row),
        stay(lengths.reshape(1, batch)),
        stay(frequency),
        stay(compressed.T),
        stay(query_up),
        stay(key_absorb),
    )
    got = swap_cores(other)
    angles = call(angle_kernel, pltpu.VMEM((3, own, 128), F32), [VMEM], name="angles")(angles)
    queries = call(
        absorb_kernel,
        shape((own * heads, WIDE), BF16),
        [VMEM] * 4 + [ANY] * 2,
        [pltpu.VMEM((own, heads, WIDE), F32)],
        name="absorb",
    )(mine, got, angles, absorb_in, stay(cache_latent), stay(cache_rope))
    queries = exchange(queries, ("x", "y", "z"))

    latent_out = call(
        attend_kernel,
        shape((groups, chips, heads, KVL), BF16),
        [SMEM, SMEM, VMEM, VMEM, VMEM],
        [pltpu.VMEM((places, 128), F32), pltpu.VMEM((128, KVL), F32)],
        limit=20,
        name="attend",
    )(
        holder,
        lengths,
        queries.reshape(groups, chips, heads, WIDE),
        keep(cache_latent),
        keep(cache_rope),
    )

    returned = exchange(latent_out.reshape(own * heads, KVL), ("x", "y", "z"))
    values = call(
        value_kernel,
        shape((own, heads * VH), BF16),
        [VMEM] * 2,
        name="values",
    )(returned, value_up)
    partial = call(
        output_kernel,
        shape((batch, out_proj.shape[1]), BF16),
        [VMEM] * 4,
        name="output",
    )(order, values, swap_cores(values), out_proj)
    partial = exchange(partial, ("x", "y"))
    partial = partial.reshape(groups, batch // groups, out_proj.shape[1])
    return jnp.sum(partial.astype(F32), axis=0).astype(BF16)


def solution(mesh):
    mesh = Mesh(mesh.devices.reshape(4, 2, 4, 4), ("z", "c", "x", "y"))
    gx, gy, both = ("z", "c"), ("x", "y"), ("z", "c", "x", "y")
    in_specs = (
        P(None, gx),
        P(gx, gy),
        P(gy, None, None),
        P(gy, None, None),
        P(gy, gx),
        P(both, None, None),
        P(both, None, None),
        P(),
        P(),
    )
    out_specs = P(gy, gx)
    return jax.shard_map(local, mesh=mesh, in_specs=in_specs, out_specs=out_specs, check_vma=False)
```

```python
import math

import jax
import jax.numpy as jnp
import numpy as np
from jax import lax
from jax.experimental import pallas as pl
from jax.experimental.pallas import tpu as pltpu
from jax.sharding import Mesh
from jax.sharding import PartitionSpec as P

KVL = 512
ROPE = 64
NOPE = 128
HEAD = NOPE + ROPE
VH = 128
WIDE = 640
SCORED = 8192
GATHERED = 16384
PARTS = 1
VMEM = pl.BlockSpec(memory_space=pltpu.VMEM)
SMEM = pl.BlockSpec(memory_space=pltpu.SMEM)
ANY = pl.BlockSpec(memory_space=pl.ANY)
F32 = jnp.float32
BF16 = jnp.bfloat16


def dot(a, b, contract_a=1, contract_b=0):
    return lax.dot_general(
        a, b, (((contract_a,), (contract_b,)), ((), ())), preferred_element_type=F32
    )


def holder_matrix(holder_row):
    count = holder_row.shape[1]
    requests = lax.broadcasted_iota(jnp.int32, (count, count), 0)
    return (requests == holder_row).astype(F32).astype(BF16)


def place_matrix(count, sending):
    row = lax.broadcasted_iota(jnp.int32, (count, count), 1)
    core = (row >> 6) ^ lax.axis_index("c")
    if sending:
        chip, group = ((row >> 4) & 3) ^ lax.axis_index("z"), row & 15
    else:
        chip, group = row & 3, (row >> 2) & 15
    slot = (chip * 2 + core) * 16 + group
    slots = lax.broadcasted_iota(jnp.int32, (count, count), 0)
    return (slots == slot).astype(F32).astype(BF16)


def project_kernel(
    holder_hbm,
    lengths_hbm,
    frequency_hbm,
    compressed_hbm,
    query_up_hbm,
    absorb_hbm,
    mine_ref,
    other_ref,
    angle_ref,
    held_ref,
    absorb_ref,
    holder,
    lengths,
    frequency,
    compressed,
    query_up,
    sems,
):
    half, width = mine_ref.shape
    part = width // PARTS
    pairs = [
        (holder_hbm, holder),
        (lengths_hbm, lengths),
        (frequency_hbm, frequency),
        (compressed_hbm, compressed),
    ]
    for i in range(PARTS):
        at = pl.ds(i * part, part)
        pairs.append((query_up_hbm.at[:, at], query_up.at[:, at]))
    pairs.append((absorb_hbm, absorb_ref))
    copies = [
        pltpu.make_async_copy(source, target, sems.at[i]) for i, (source, target) in enumerate(pairs)
    ]
    for copy in copies:
        copy.start()
    for copy in copies[:3]:
        copy.wait()
    held = holder_matrix(holder[...])
    held_ref[...] = held
    place = place_matrix(held.shape[0], True)
    order = dot(held, place).astype(BF16)
    turned = dot(place, held, 0, 1)[: angle_ref.shape[0]]
    last = jnp.sum(turned * (lengths[...] - 1).astype(F32), axis=1, keepdims=True)
    angle_ref[...] = last * frequency[...]
    copies[3].wait()
    by_slot = dot(compressed[...], order).astype(BF16)
    for i in range(PARTS):
        at = slice(i * part, i * part + part)
        copies[4 + i].wait()
        term = dot(by_slot, query_up[:, at], 0, 0)
        mine_ref[:, at] = term[:half]
        other_ref[:, at] = term[half:].astype(BF16)
    copies[-1].wait()


def angle_kernel(angle_ref, held_ref, latent_hbm, rope_hbm, out_ref, order_ref):
    angles = angle_ref[...]
    sin = jnp.sin(angles)
    lane = lax.broadcasted_iota(jnp.int32, angles.shape, 1)
    former = (lane & (ROPE - 1)) < ROPE // 2
    out_ref[0] = jnp.cos(angles)
    out_ref[1] = jnp.where(former, -sin, 0.0)
    out_ref[2] = jnp.where(former, 0.0, sin)
    held = held_ref[...]
    order_ref[...] = dot(held, place_matrix(held.shape[0], False)).astype(BF16)


def pair_kernel(mine_ref, got_ref, own_ref, one_ref, two_ref, three_ref):
    rows = own_ref.shape[0]
    for k, out_ref in enumerate((own_ref, one_ref, two_ref, three_ref)):
        at = slice(k * rows, k * rows + rows)
        out_ref[...] = (mine_ref[at] + got_ref[at].astype(F32)).astype(out_ref.dtype)


def absorb_kernel(
    own_ref, one_ref, two_ref, three_ref, angle_ref, absorb_ref, out_ref, wide_ref
):
    queries = (
        own_ref[...]
        + one_ref[...].astype(F32)
        + two_ref[...].astype(F32)
        + three_ref[...].astype(F32)
    )
    lane = lax.broadcasted_iota(jnp.int32, (queries.shape[0], 128), 1)
    low = lane < 64
    for h in range(0, absorb_ref.shape[0], 2):
        start = h * HEAD
        first = queries[:, start : start + 128]
        second = queries[:, start + 128 : start + 256]
        third = queries[:, start + 256 : start + 384]
        other = pltpu.roll(jnp.where(low, third, second), 64, 1)
        rope = jnp.where(low, second, third)
        rope = (
            rope * angle_ref[0]
            + pltpu.roll(rope, 128 - ROPE // 2, 1) * angle_ref[1]
            + pltpu.roll(rope, ROPE // 2, 1) * angle_ref[2]
        )
        wide_ref[:, h, :KVL] = dot(first.astype(BF16), absorb_ref[h])
        wide_ref[:, h, KVL:] = jnp.where(low, rope, 0.0)
        wide_ref[:, h + 1, :KVL] = dot(other.astype(BF16), absorb_ref[h + 1])
        wide_ref[:, h + 1, KVL:] = jnp.where(low, 0.0, rope)
    out_ref[...] = wide_ref[...].reshape(out_ref.shape).astype(BF16)


def attend_kernel(holder_ref, lengths_ref, query_ref, latent, rope, out_ref, scores, acc):
    slot = (lax.axis_index("z") * 2 + lax.axis_index("c")) * 16
    slot += lax.axis_index("x") * 4 + lax.axis_index("y")
    length = lengths_ref[holder_ref[slot]]
    places = latent.shape[1]
    groups, chips, heads = out_ref.shape[:3]
    count = groups * heads

    query = query_ref[...].astype(F32) * (math.log2(math.e) / math.sqrt(HEAD))
    query_lat = query[:, :KVL].astype(BF16)
    query_rope = (query[:, KVL : KVL + ROPE] + query[:, KVL + ROPE :]).astype(BF16)

    def score(i, top):
        start = pl.multiple_of(i * SCORED, SCORED)
        at = pl.ds(start, SCORED)
        s = dot(latent[0, at, :], query_lat, 1, 1) + dot(rope[0, :, at], query_rope, 0, 1)
        position = start + lax.broadcasted_iota(jnp.int32, s.shape, 0)
        s = jnp.where(position < length, s, -1e30)
        scores[at, :] = s
        return jnp.maximum(top, jnp.max(s, axis=0, keepdims=True))

    top = lax.fori_loop(0, places // SCORED, score, jnp.full((1, count), -1e30, F32))
    acc[...] = jnp.zeros(acc.shape, F32)

    def gather(i, total):
        at = pl.ds(pl.multiple_of(i * GATHERED, GATHERED), GATHERED)
        p = jnp.exp2(scores[at, :] - top)
        acc[...] += dot(p.astype(BF16), latent[0, at, :], 0, 0)
        return total + jnp.sum(p, axis=0, keepdims=True)

    total = lax.fori_loop(0, places // GATHERED, gather, jnp.zeros((1, count), F32))
    total = jnp.transpose(jnp.broadcast_to(total, (count, count)))[:, :1]
    result = (acc[...] / total).reshape(groups, heads, KVL).astype(BF16)
    for z in range(chips):
        out_ref[:, z] = result


def value_kernel(latent_ref, value_up_ref, out_ref):
    heads = value_up_ref.shape[0]
    rows = latent_ref.shape[0]
    slots = rows // heads
    row = lax.broadcasted_iota(jnp.int32, (rows, rows), 0)
    came = lax.broadcasted_iota(jnp.int32, (rows, rows), 1)
    by_head = ((row % slots) * heads + row // slots == came).astype(F32).astype(BF16)
    latents = dot(by_head, latent_ref[...]).astype(BF16)
    for h in range(heads):
        out_ref[:, h * VH : h * VH + VH] = dot(
            latents[h * slots : h * slots + slots], value_up_ref[h]
        ).astype(BF16)


def output_kernel(order_ref, own_ref, pair_ref, proj_ref, out_ref):
    values = jnp.concatenate([own_ref[...], pair_ref[...]], axis=0)
    values = dot(order_ref[...], values).astype(BF16)
    out_ref[...] = dot(values, proj_ref[...]).astype(BF16)


def call(kernel, out_shape, in_specs, scratch=(), limit=8, name=None, cost=None):
    many = isinstance(out_shape, (list, tuple))
    return pl.pallas_call(
        kernel,
        out_shape=out_shape,
        in_specs=in_specs,
        out_specs=[VMEM] * len(out_shape) if many else VMEM,
        scratch_shapes=list(scratch),
        compiler_params=pltpu.CompilerParams(vmem_limit_bytes=limit * 2**20),
        name=name,
        cost_estimate=cost,
    )


def stay(array):
    return pltpu.with_memory_space_constraint(array, pltpu.HBM)


def keep(array):
    return pltpu.with_memory_space_constraint(array, pltpu.VMEM)


def swap_cores(array):
    return lax.ppermute(array, "c", [(0, 1), (1, 0)])


def swap_chips(array, distance):
    return lax.ppermute(array, "z", [(i, i ^ distance) for i in range(lax.axis_size("z"))])


def exchange(array, axes):
    return lax.all_to_all(array, axes, split_axis=0, concat_axis=0, tiled=True)


def local(
    compressed, query_up, key_absorb, value_up, out_proj, cache_latent, cache_rope, lengths, holder
):
    shape = jax.ShapeDtypeStruct
    batch = compressed.shape[0]
    width = query_up.shape[1]
    heads = key_absorb.shape[0]
    places = cache_latent.shape[1]
    chips = lax.axis_size("z")
    groups = lax.axis_size("x") * lax.axis_size("y")
    own = chips * groups
    holder_row = holder.reshape(1, batch)
    half = np.arange(ROPE // 2, dtype=np.float32)
    frequency = (10000.0 ** (-2.0 * half / ROPE)).astype(np.float32)
    frequency = jnp.asarray(np.tile(frequency, 4)[None, :])

    mine, other, angles, held, absorb_in = call(
        project_kernel,
        (
            pltpu.VMEM((own, width), F32),
            pltpu.VMEM((own, width), BF16),
            pltpu.VMEM((groups, 128), F32),
            pltpu.VMEM((batch, batch), BF16),
            pltpu.VMEM(key_absorb.shape, BF16),
        ),
        [ANY] * 6,
        [
            pltpu.VMEM((1, batch), jnp.int32),
            pltpu.VMEM((1, batch), jnp.int32),
            pltpu.VMEM((1, 128), F32),
            pltpu.VMEM((compressed.shape[1], batch), BF16),
            pltpu.VMEM(query_up.shape, BF16),
            pltpu.SemaphoreType.DMA((5 + PARTS,)),
        ],
        name="project",
    )(
        stay(holder_row),
        stay(lengths.reshape(1, batch)),
        stay(frequency),
        stay(compressed.T),
        stay(query_up),
        stay(key_absorb),
    )
    got = swap_cores(other)
    angles, order = call(
        angle_kernel,
        (pltpu.VMEM((3, groups, 128), F32), pltpu.VMEM((batch, batch), BF16)),
        [VMEM] * 2 + [ANY] * 2,
        name="angles",
    )(angles, held, stay(cache_latent), stay(cache_rope))
    part = shape((groups, width), BF16)
    mine, one, two, three = call(
        pair_kernel,
        (shape((groups, width), F32), part, part, part),
        [VMEM] * 2,
        name="pair",
    )(mine, got)
    one, two, three = (swap_chips(array, k + 1) for k, array in enumerate((one, two, three)))
    queries = call(
        absorb_kernel,
        shape((groups * heads, WIDE), BF16),
        [VMEM] * 6,
        [pltpu.VMEM((groups, heads, WIDE), F32)],
        name="absorb",
    )(mine, one, two, three, angles, absorb_in)
    queries = exchange(queries, ("x", "y"))

    latent_out = call(
        attend_kernel,
        shape((groups, chips, heads, KVL), BF16),
        [SMEM, SMEM, VMEM, VMEM, VMEM],
        [pltpu.VMEM((places, 128), F32), pltpu.VMEM((128, KVL), F32)],
        limit=20,
        name="attend",
    )(holder, lengths, queries, keep(cache_latent), keep(cache_rope))

    returned = exchange(latent_out.reshape(own * heads, KVL), ("x", "y", "z"))
    values = call(
        value_kernel,
        shape((own, heads * VH), BF16),
        [VMEM] * 2,
        name="values",
    )(returned, value_up)
    partial = call(
        output_kernel,
        shape((batch, out_proj.shape[1]), BF16),
        [VMEM] * 4,
        name="output",
    )(order, values, swap_cores(values), out_proj)
    partial = exchange(partial, ("x", "y"))
    partial = partial.reshape(groups, batch // groups, out_proj.shape[1])
    return jnp.sum(partial.astype(F32), axis=0).astype(BF16)


def solution(mesh):
    mesh = Mesh(mesh.devices.reshape(4, 2, 4, 4), ("z", "c", "x", "y"))
    gx, gy, both = ("z", "c"), ("x", "y"), ("z", "c", "x", "y")
    in_specs = (
        P(None, gx),
        P(gx, gy),
        P(gy, None, None),
        P(gy, None, None),
        P(gy, gx),
        P(both, None, None),
        P(both, None, None),
        P(),
        P(),
    )
    out_specs = P(gy, gx)
    return jax.shard_map(local, mesh=mesh, in_specs=in_specs, out_specs=out_specs, check_vma=False)
```

```python
import math

import jax
import jax.numpy as jnp
import numpy as np
from jax import lax
from jax.experimental import pallas as pl
from jax.experimental.pallas import tpu as pltpu
from jax.sharding import Mesh
from jax.sharding import PartitionSpec as P

KVL = 512
ROPE = 64
NOPE = 128
HEAD = NOPE + ROPE
VH = 128
WIDE = 640
SCORED = 8192
GATHERED = 16384
PARTS = 2
VMEM = pl.BlockSpec(memory_space=pltpu.VMEM)
SMEM = pl.BlockSpec(memory_space=pltpu.SMEM)
ANY = pl.BlockSpec(memory_space=pl.ANY)
F32 = jnp.float32
BF16 = jnp.bfloat16


def dot(a, b, contract_a=1, contract_b=0):
    return lax.dot_general(
        a, b, (((contract_a,), (contract_b,)), ((), ())), preferred_element_type=F32
    )


def holder_matrix(holder_row):
    count = holder_row.shape[1]
    requests = lax.broadcasted_iota(jnp.int32, (count, count), 0)
    return (requests == holder_row).astype(F32).astype(BF16)


def place_matrix(count, sending):
    row = lax.broadcasted_iota(jnp.int32, (count, count), 1)
    core = (row >> 6) ^ lax.axis_index("c")
    if sending:
        chip, group = ((row >> 4) & 3) ^ lax.axis_index("z"), row & 15
    else:
        chip, group = row & 3, (row >> 2) & 15
    slot = (chip * 2 + core) * 16 + group
    slots = lax.broadcasted_iota(jnp.int32, (count, count), 0)
    return (slots == slot).astype(F32).astype(BF16)


def project_kernel(
    holder_hbm,
    lengths_hbm,
    frequency_hbm,
    compressed_hbm,
    query_up_hbm,
    absorb_hbm,
    other_ref,
    held_ref,
    lengths_ref,
    frequency_ref,
    by_slot_ref,
    query_up_ref,
    holder,
    compressed,
    sems,
):
    half = other_ref.shape[0]
    depth = query_up_ref.shape[0] // PARTS
    pairs = [(holder_hbm, holder), (compressed_hbm, compressed)]
    for i in range(PARTS):
        at = pl.ds(i * depth, depth)
        pairs.append((query_up_hbm.at[at, :], query_up_ref.at[at, :]))
    pairs += [(lengths_hbm, lengths_ref), (frequency_hbm, frequency_ref)]
    copies = [
        pltpu.make_async_copy(source, target, sems.at[i]) for i, (source, target) in enumerate(pairs)
    ]
    for copy in copies:
        copy.start()
    copies[0].wait()
    held = holder_matrix(holder[...])
    held_ref[...] = held
    order = dot(held, place_matrix(held.shape[0], True)).astype(BF16)
    copies[1].wait()
    by_slot = dot(compressed[...], order).astype(BF16)
    by_slot_ref[...] = by_slot
    for copy in copies[2:]:
        copy.wait()
    other_ref[...] = dot(by_slot[:, half:], query_up_ref[...], 0, 0).astype(BF16)


def mine_kernel(by_slot_ref, query_up_ref, held_ref, lengths_ref, frequency_ref, mine_ref, angle_ref):
    mine_ref[...] = dot(by_slot_ref[:, : mine_ref.shape[0]], query_up_ref[...], 0, 0)
    held = held_ref[...]
    place = place_matrix(held.shape[0], True)
    turned = dot(place, held, 0, 1)[: angle_ref.shape[0]]
    last = jnp.sum(turned * (lengths_ref[...] - 1).astype(F32), axis=1, keepdims=True)
    angle_ref[...] = last * frequency_ref[...]


def angle_kernel(angle_ref, held_ref, latent_hbm, rope_hbm, out_ref, order_ref):
    angles = angle_ref[...]
    sin = jnp.sin(angles)
    lane = lax.broadcasted_iota(jnp.int32, angles.shape, 1)
    former = (lane & (ROPE - 1)) < ROPE // 2
    out_ref[0] = jnp.cos(angles)
    out_ref[1] = jnp.where(former, -sin, 0.0)
    out_ref[2] = jnp.where(former, 0.0, sin)
    held = held_ref[...]
    order_ref[...] = dot(held, place_matrix(held.shape[0], False)).astype(BF16)


def pair_kernel(mine_ref, got_ref, own_ref, one_ref, two_ref, three_ref):
    rows = own_ref.shape[0]
    for k, out_ref in enumerate((own_ref, one_ref, two_ref, three_ref)):
        at = slice(k * rows, k * rows + rows)
        out_ref[...] = (mine_ref[at] + got_ref[at].astype(F32)).astype(out_ref.dtype)


def absorb_kernel(
    own_ref, two_ref, one_ref, three_ref, angle_ref, absorb_ref, out_ref, wide_ref
):
    queries = (
        own_ref[...]
        + one_ref[...].astype(F32)
        + two_ref[...].astype(F32)
        + three_ref[...].astype(F32)
    )
    lane = lax.broadcasted_iota(jnp.int32, (queries.shape[0], 128), 1)
    low = lane < 64
    for h in range(0, absorb_ref.shape[0], 2):
        start = h * HEAD
        first = queries[:, start : start + 128]
        second = queries[:, start + 128 : start + 256]
        third = queries[:, start + 256 : start + 384]
        other = pltpu.roll(jnp.where(low, third, second), 64, 1)
        rope = jnp.where(low, second, third)
        rope = (
            rope * angle_ref[0]
            + pltpu.roll(rope, 128 - ROPE // 2, 1) * angle_ref[1]
            + pltpu.roll(rope, ROPE // 2, 1) * angle_ref[2]
        )
        wide_ref[:, h, :KVL] = dot(first.astype(BF16), absorb_ref[h])
        wide_ref[:, h, KVL:] = jnp.where(low, rope, 0.0)
        wide_ref[:, h + 1, :KVL] = dot(other.astype(BF16), absorb_ref[h + 1])
        wide_ref[:, h + 1, KVL:] = jnp.where(low, 0.0, rope)
    out_ref[...] = wide_ref[...].reshape(out_ref.shape).astype(BF16)


def attend_kernel(holder_ref, lengths_ref, query_ref, latent, rope, out_ref, scores, acc):
    slot = (lax.axis_index("z") * 2 + lax.axis_index("c")) * 16
    slot += lax.axis_index("x") * 4 + lax.axis_index("y")
    length = lengths_ref[holder_ref[slot]]
    places = latent.shape[1]
    groups, chips, heads = out_ref.shape[:3]
    count = groups * heads

    query = query_ref[...].astype(F32) * (math.log2(math.e) / math.sqrt(HEAD))
    query_lat = query[:, :KVL].astype(BF16)
    query_rope = (query[:, KVL : KVL + ROPE] + query[:, KVL + ROPE :]).astype(BF16)

    def score(i, top):
        start = pl.multiple_of(i * SCORED, SCORED)
        at = pl.ds(start, SCORED)
        s = dot(latent[0, at, :], query_lat, 1, 1) + dot(rope[0, :, at], query_rope, 0, 1)
        position = start + lax.broadcasted_iota(jnp.int32, s.shape, 0)
        s = jnp.where(position < length, s, -1e30)
        scores[at, :] = s
        return jnp.maximum(top, jnp.max(s, axis=0, keepdims=True))

    top = lax.fori_loop(0, places // SCORED, score, jnp.full((1, count), -1e30, F32))
    acc[...] = jnp.zeros(acc.shape, F32)

    def gather(i, total):
        at = pl.ds(pl.multiple_of(i * GATHERED, GATHERED), GATHERED)
        p = jnp.exp2(scores[at, :] - top)
        acc[...] += dot(p.astype(BF16), latent[0, at, :], 0, 0)
        return total + jnp.sum(p, axis=0, keepdims=True)

    total = lax.fori_loop(0, places // GATHERED, gather, jnp.zeros((1, count), F32))
    total = jnp.transpose(jnp.broadcast_to(total, (count, count)))[:, :1]
    result = (acc[...] / total).reshape(groups, heads, KVL).astype(BF16)
    for z in range(chips):
        out_ref[:, z] = result


def value_kernel(latent_ref, value_up_ref, out_ref):
    heads = value_up_ref.shape[0]
    rows = latent_ref.shape[0]
    slots = rows // heads
    row = lax.broadcasted_iota(jnp.int32, (rows, rows), 0)
    came = lax.broadcasted_iota(jnp.int32, (rows, rows), 1)
    by_head = ((row % slots) * heads + row // slots == came).astype(F32).astype(BF16)
    latents = dot(by_head, latent_ref[...]).astype(BF16)
    for h in range(heads):
        out_ref[:, h * VH : h * VH + VH] = dot(
            latents[h * slots : h * slots + slots], value_up_ref[h]
        ).astype(BF16)


def output_kernel(order_ref, own_ref, pair_ref, proj_ref, out_ref):
    values = jnp.concatenate([own_ref[...], pair_ref[...]], axis=0)
    values = dot(order_ref[...], values).astype(BF16)
    out_ref[...] = dot(values, proj_ref[...]).astype(BF16)


def call(kernel, out_shape, in_specs, scratch=(), limit=8, name=None, cost=None):
    many = isinstance(out_shape, (list, tuple))
    return pl.pallas_call(
        kernel,
        out_shape=out_shape,
        in_specs=in_specs,
        out_specs=[VMEM] * len(out_shape) if many else VMEM,
        scratch_shapes=list(scratch),
        compiler_params=pltpu.CompilerParams(vmem_limit_bytes=limit * 2**20),
        name=name,
        cost_estimate=cost,
    )


def stay(array):
    return pltpu.with_memory_space_constraint(array, pltpu.HBM)


def keep(array):
    return pltpu.with_memory_space_constraint(array, pltpu.VMEM)


def swap_cores(array):
    return lax.ppermute(array, "c", [(0, 1), (1, 0)])


def swap_chips(array, distance):
    return lax.ppermute(array, "z", [(i, i ^ distance) for i in range(lax.axis_size("z"))])


def exchange(array, axes):
    return lax.all_to_all(array, axes, split_axis=0, concat_axis=0, tiled=True)


def local(
    compressed, query_up, key_absorb, value_up, out_proj, cache_latent, cache_rope, lengths, holder
):
    shape = jax.ShapeDtypeStruct
    batch = compressed.shape[0]
    width = query_up.shape[1]
    heads = key_absorb.shape[0]
    places = cache_latent.shape[1]
    chips = lax.axis_size("z")
    groups = lax.axis_size("x") * lax.axis_size("y")
    own = chips * groups
    holder_row = holder.reshape(1, batch)
    half = np.arange(ROPE // 2, dtype=np.float32)
    frequency = (10000.0 ** (-2.0 * half / ROPE)).astype(np.float32)
    frequency = jnp.asarray(np.tile(frequency, 4)[None, :])

    other, held, lengths_row, frequency, by_slot, weights = call(
        project_kernel,
        (
            pltpu.VMEM((own, width), BF16),
            pltpu.VMEM((batch, batch), BF16),
            pltpu.VMEM((1, batch), jnp.int32),
            pltpu.VMEM((1, 128), F32),
            pltpu.VMEM((compressed.shape[1], batch), BF16),
            pltpu.VMEM(query_up.shape, BF16),
        ),
        [ANY] * 6,
        [
            pltpu.VMEM((1, batch), jnp.int32),
            pltpu.VMEM((compressed.shape[1], batch), BF16),
            pltpu.SemaphoreType.DMA((4 + PARTS,)),
        ],
        name="project",
    )(
        stay(holder_row),
        stay(lengths.reshape(1, batch)),
        stay(frequency),
        stay(compressed.T),
        stay(query_up),
        stay(key_absorb),
    )
    got = swap_cores(other)
    mine, angles = call(
        mine_kernel,
        (pltpu.VMEM((own, width), F32), pltpu.VMEM((groups, 128), F32)),
        [VMEM] * 5,
        name="mine",
    )(by_slot, weights, held, lengths_row, frequency)
    angles, order = call(
        angle_kernel,
        (pltpu.VMEM((3, groups, 128), F32), pltpu.VMEM((batch, batch), BF16)),
        [VMEM] * 2 + [ANY] * 2,
        name="angles",
    )(angles, held, stay(cache_latent), stay(cache_rope))
    part = shape((groups, width), BF16)
    mine, one, two, three = call(
        pair_kernel,
        (shape((groups, width), F32), part, part, part),
        [VMEM] * 2,
        name="pair",
    )(mine, got)
    one, two, three = (swap_chips(array, k + 1) for k, array in enumerate((one, two, three)))
    queries = call(
        absorb_kernel,
        shape((groups * heads, WIDE), BF16),
        [VMEM] * 6,
        [pltpu.VMEM((groups, heads, WIDE), F32)],
        name="absorb",
    )(mine, two, one, three, angles, keep(key_absorb))
    queries = exchange(queries, ("x", "y"))

    latent_out = call(
        attend_kernel,
        shape((groups, chips, heads, KVL), BF16),
        [SMEM, SMEM, VMEM, VMEM, VMEM],
        [pltpu.VMEM((places, 128), F32), pltpu.VMEM((128, KVL), F32)],
        limit=20,
        name="attend",
    )(holder, lengths, queries, keep(cache_latent), keep(cache_rope))

    returned = exchange(latent_out.reshape(own * heads, KVL), ("x", "y", "z"))
    values = call(
        value_kernel,
        shape((own, heads * VH), BF16),
        [VMEM] * 2,
        name="values",
    )(returned, value_up)
    partial = call(
        output_kernel,
        shape((batch, out_proj.shape[1]), BF16),
        [VMEM] * 4,
        name="output",
    )(order, values, swap_cores(values), out_proj)
    partial = exchange(partial, ("x", "y"))
    partial = partial.reshape(groups, batch // groups, out_proj.shape[1])
    return jnp.sum(partial.astype(F32), axis=0).astype(BF16)


def solution(mesh):
    mesh = Mesh(mesh.devices.reshape(4, 2, 4, 4), ("z", "c", "x", "y"))
    gx, gy, both = ("z", "c"), ("x", "y"), ("z", "c", "x", "y")
    in_specs = (
        P(None, gx),
        P(gx, gy),
        P(gy, None, None),
        P(gy, None, None),
        P(gy, gx),
        P(both, None, None),
        P(both, None, None),
        P(),
        P(),
    )
    out_specs = P(gy, gx)
    return jax.shard_map(local, mesh=mesh, in_specs=in_specs, out_specs=out_specs, check_vma=False)
```

```python
import math

import jax
import jax.numpy as jnp
import numpy as np
from jax import lax
from jax.experimental import pallas as pl
from jax.experimental.pallas import tpu as pltpu
from jax.sharding import Mesh
from jax.sharding import PartitionSpec as P

KVL = 512
ROPE = 64
NOPE = 128
HEAD = NOPE + ROPE
VH = 128
WIDE = 640
SCORED = 8192
GATHERED = 16384
PARTS = 2
VMEM = pl.BlockSpec(memory_space=pltpu.VMEM)
SMEM = pl.BlockSpec(memory_space=pltpu.SMEM)
ANY = pl.BlockSpec(memory_space=pl.ANY)
F32 = jnp.float32
BF16 = jnp.bfloat16


def dot(a, b, contract_a=1, contract_b=0):
    return lax.dot_general(
        a, b, (((contract_a,), (contract_b,)), ((), ())), preferred_element_type=F32
    )


def holder_matrix(holder_row):
    count = holder_row.shape[1]
    requests = lax.broadcasted_iota(jnp.int32, (count, count), 0)
    return (requests == holder_row).astype(F32).astype(BF16)


def place_matrix(count, sending):
    row = lax.broadcasted_iota(jnp.int32, (count, count), 1)
    core = (row >> 6) ^ lax.axis_index("c")
    if sending:
        chip, group = ((row >> 4) & 3) ^ lax.axis_index("z"), row & 15
    else:
        chip, group = row & 3, (row >> 2) & 15
    slot = (chip * 2 + core) * 16 + group
    slots = lax.broadcasted_iota(jnp.int32, (count, count), 0)
    return (slots == slot).astype(F32).astype(BF16)


def project_kernel(
    holder_hbm,
    lengths_hbm,
    frequency_hbm,
    compressed_hbm,
    query_up_hbm,
    absorb_hbm,
    other_ref,
    held_ref,
    lengths_ref,
    frequency_ref,
    by_slot_ref,
    query_up_ref,
    holder,
    compressed,
    sems,
):
    half = other_ref.shape[0]
    depth = query_up_ref.shape[0] // PARTS
    pairs = [(holder_hbm, holder), (compressed_hbm, compressed)]
    for i in range(PARTS):
        at = pl.ds(i * depth, depth)
        pairs.append((query_up_hbm.at[at, :], query_up_ref.at[at, :]))
    pairs += [(lengths_hbm, lengths_ref), (frequency_hbm, frequency_ref)]
    copies = [
        pltpu.make_async_copy(source, target, sems.at[i]) for i, (source, target) in enumerate(pairs)
    ]
    for copy in copies:
        copy.start()
    copies[0].wait()
    held = holder_matrix(holder[...])
    held_ref[...] = held
    order = dot(held, place_matrix(held.shape[0], True)).astype(BF16)
    copies[1].wait()
    by_slot = dot(compressed[...], order).astype(BF16)
    by_slot_ref[...] = by_slot
    for copy in copies[2:]:
        copy.wait()
    other_ref[...] = dot(by_slot[:, half:], query_up_ref[...], 0, 0).astype(BF16)


def mine_kernel(by_slot_ref, query_up_ref, held_ref, lengths_ref, frequency_ref, mine_ref, angle_ref):
    mine_ref[...] = dot(by_slot_ref[:, : mine_ref.shape[0]], query_up_ref[...], 0, 0)
    held = held_ref[...]
    place = place_matrix(held.shape[0], True)
    turned = dot(place, held, 0, 1)[: angle_ref.shape[0]]
    last = jnp.sum(turned * (lengths_ref[...] - 1).astype(F32), axis=1, keepdims=True)
    angle_ref[...] = last * frequency_ref[...]


def angle_kernel(angle_ref, held_ref, latent_hbm, rope_hbm, out_ref, order_ref, regroup_ref):
    angles = angle_ref[...]
    sin = jnp.sin(angles)
    lane = lax.broadcasted_iota(jnp.int32, angles.shape, 1)
    former = (lane & (ROPE - 1)) < ROPE // 2
    out_ref[0] = jnp.cos(angles)
    out_ref[1] = jnp.where(former, -sin, 0.0)
    out_ref[2] = jnp.where(former, 0.0, sin)
    held = held_ref[...]
    order_ref[...] = dot(held, place_matrix(held.shape[0], False)).astype(BF16)
    rows, slots = regroup_ref.shape[0], held.shape[0] // 2
    row = lax.broadcasted_iota(jnp.int32, (rows, rows), 0)
    came = lax.broadcasted_iota(jnp.int32, (rows, rows), 1)
    by_head = (row % slots) * (rows // slots) + row // slots == came
    regroup_ref[...] = by_head.astype(F32).astype(BF16)


def pair_kernel(mine_ref, got_ref, own_ref, one_ref, two_ref, three_ref):
    rows = own_ref.shape[0]
    for k, out_ref in enumerate((own_ref, one_ref, two_ref, three_ref)):
        at = slice(k * rows, k * rows + rows)
        out_ref[...] = (mine_ref[at] + got_ref[at].astype(F32)).astype(out_ref.dtype)


def absorb_kernel(
    own_ref, two_ref, one_ref, three_ref, angle_ref, absorb_ref, out_ref, wide_ref
):
    queries = (
        own_ref[...]
        + one_ref[...].astype(F32)
        + two_ref[...].astype(F32)
        + three_ref[...].astype(F32)
    )
    lane = lax.broadcasted_iota(jnp.int32, (queries.shape[0], 128), 1)
    low = lane < 64
    for h in range(0, absorb_ref.shape[0], 2):
        start = h * HEAD
        first = queries[:, start : start + 128]
        second = queries[:, start + 128 : start + 256]
        third = queries[:, start + 256 : start + 384]
        other = pltpu.roll(jnp.where(low, third, second), 64, 1)
        rope = jnp.where(low, second, third)
        rope = (
            rope * angle_ref[0]
            + pltpu.roll(rope, 128 - ROPE // 2, 1) * angle_ref[1]
            + pltpu.roll(rope, ROPE // 2, 1) * angle_ref[2]
        )
        wide_ref[:, h, :KVL] = dot(first.astype(BF16), absorb_ref[h])
        wide_ref[:, h, KVL:] = jnp.where(low, rope, 0.0)
        wide_ref[:, h + 1, :KVL] = dot(other.astype(BF16), absorb_ref[h + 1])
        wide_ref[:, h + 1, KVL:] = jnp.where(low, 0.0, rope)
    out_ref[...] = wide_ref[...].reshape(out_ref.shape).astype(BF16)


def attend_kernel(holder_ref, lengths_ref, query_ref, latent, rope, out_ref, scores, acc):
    slot = (lax.axis_index("z") * 2 + lax.axis_index("c")) * 16
    slot += lax.axis_index("x") * 4 + lax.axis_index("y")
    length = lengths_ref[holder_ref[slot]]
    places = latent.shape[1]
    groups, chips, heads = out_ref.shape[:3]
    count = groups * heads

    query = query_ref[...].astype(F32) * (math.log2(math.e) / math.sqrt(HEAD))
    query_lat = query[:, :KVL].astype(BF16)
    query_rope = (query[:, KVL : KVL + ROPE] + query[:, KVL + ROPE :]).astype(BF16)

    def score(i, top):
        start = pl.multiple_of(i * SCORED, SCORED)
        at = pl.ds(start, SCORED)
        s = dot(latent[0, at, :], query_lat, 1, 1) + dot(rope[0, :, at], query_rope, 0, 1)
        position = start + lax.broadcasted_iota(jnp.int32, s.shape, 0)
        s = jnp.where(position < length, s, -1e30)
        scores[at, :] = s
        return jnp.maximum(top, jnp.max(s, axis=0, keepdims=True))

    top = lax.fori_loop(0, places // SCORED, score, jnp.full((1, count), -1e30, F32))
    acc[...] = jnp.zeros(acc.shape, F32)

    def gather(i, total):
        at = pl.ds(pl.multiple_of(i * GATHERED, GATHERED), GATHERED)
        p = jnp.exp2(scores[at, :] - top)
        acc[...] += dot(p.astype(BF16), latent[0, at, :], 0, 0)
        return total + jnp.sum(p, axis=0, keepdims=True)

    total = lax.fori_loop(0, places // GATHERED, gather, jnp.zeros((1, count), F32))
    total = jnp.transpose(jnp.broadcast_to(total, (count, count)))[:, :1]
    result = (acc[...] / total).reshape(groups, heads, KVL).astype(BF16)
    for z in range(chips):
        out_ref[:, z] = result


def value_kernel(regroup_ref, latent_ref, value_up_ref, out_ref):
    heads = value_up_ref.shape[0]
    rows = latent_ref.shape[0]
    slots = rows // heads
    latents = dot(regroup_ref[...], latent_ref[...]).astype(BF16)
    for h in range(heads):
        out_ref[:, h * VH : h * VH + VH] = dot(
            latents[h * slots : h * slots + slots], value_up_ref[h]
        ).astype(BF16)


def output_kernel(order_ref, own_ref, pair_ref, proj_ref, out_ref):
    values = jnp.concatenate([own_ref[...], pair_ref[...]], axis=0)
    values = dot(order_ref[...], values).astype(BF16)
    out_ref[...] = dot(values, proj_ref[...]).astype(BF16)


def call(kernel, out_shape, in_specs, scratch=(), limit=8, name=None, cost=None):
    many = isinstance(out_shape, (list, tuple))
    return pl.pallas_call(
        kernel,
        out_shape=out_shape,
        in_specs=in_specs,
        out_specs=[VMEM] * len(out_shape) if many else VMEM,
        scratch_shapes=list(scratch),
        compiler_params=pltpu.CompilerParams(vmem_limit_bytes=limit * 2**20),
        name=name,
        cost_estimate=cost,
    )


def stay(array):
    return pltpu.with_memory_space_constraint(array, pltpu.HBM)


def keep(array):
    return pltpu.with_memory_space_constraint(array, pltpu.VMEM)


def swap_cores(array):
    return lax.ppermute(array, "c", [(0, 1), (1, 0)])


def swap_chips(array, distance):
    return lax.ppermute(array, "z", [(i, i ^ distance) for i in range(lax.axis_size("z"))])


def exchange(array, axes):
    return lax.all_to_all(array, axes, split_axis=0, concat_axis=0, tiled=True)


def local(
    compressed, query_up, key_absorb, value_up, out_proj, cache_latent, cache_rope, lengths, holder
):
    shape = jax.ShapeDtypeStruct
    batch = compressed.shape[0]
    width = query_up.shape[1]
    heads = key_absorb.shape[0]
    places = cache_latent.shape[1]
    chips = lax.axis_size("z")
    groups = lax.axis_size("x") * lax.axis_size("y")
    own = chips * groups
    holder_row = holder.reshape(1, batch)
    half = np.arange(ROPE // 2, dtype=np.float32)
    frequency = (10000.0 ** (-2.0 * half / ROPE)).astype(np.float32)
    frequency = jnp.asarray(np.tile(frequency, 4)[None, :])

    other, held, lengths_row, frequency, by_slot, weights = call(
        project_kernel,
        (
            pltpu.VMEM((own, width), BF16),
            pltpu.VMEM((batch, batch), BF16),
            pltpu.VMEM((1, batch), jnp.int32),
            pltpu.VMEM((1, 128), F32),
            pltpu.VMEM((compressed.shape[1], batch), BF16),
            pltpu.VMEM(query_up.shape, BF16),
        ),
        [ANY] * 6,
        [
            pltpu.VMEM((1, batch), jnp.int32),
            pltpu.VMEM((compressed.shape[1], batch), BF16),
            pltpu.SemaphoreType.DMA((4 + PARTS,)),
        ],
        name="project",
    )(
        stay(holder_row),
        stay(lengths.reshape(1, batch)),
        stay(frequency),
        stay(compressed.T),
        stay(query_up),
        stay(key_absorb),
    )
    got = swap_cores(other)
    mine, angles = call(
        mine_kernel,
        (pltpu.VMEM((own, width), F32), pltpu.VMEM((groups, 128), F32)),
        [VMEM] * 5,
        name="mine",
    )(by_slot, weights, held, lengths_row, frequency)
    angles, order, regroup = call(
        angle_kernel,
        (
            pltpu.VMEM((3, groups, 128), F32),
            pltpu.VMEM((batch, batch), BF16),
            pltpu.VMEM((own * heads, own * heads), BF16),
        ),
        [VMEM] * 2 + [ANY] * 2,
        name="angles",
    )(angles, held, stay(cache_latent), stay(cache_rope))
    part = shape((groups, width), BF16)
    mine, one, two, three = call(
        pair_kernel,
        (shape((groups, width), F32), part, part, part),
        [VMEM] * 2,
        name="pair",
    )(mine, got)
    one, two, three = (swap_chips(array, k + 1) for k, array in enumerate((one, two, three)))
    queries = call(
        absorb_kernel,
        shape((groups * heads, WIDE), BF16),
        [VMEM] * 6,
        [pltpu.VMEM((groups, heads, WIDE), F32)],
        name="absorb",
    )(mine, two, one, three, angles, keep(key_absorb))
    queries = exchange(queries, ("x", "y"))

    latent_out = call(
        attend_kernel,
        shape((groups, chips, heads, KVL), BF16),
        [SMEM, SMEM, VMEM, VMEM, VMEM],
        [pltpu.VMEM((places, 128), F32), pltpu.VMEM((128, KVL), F32)],
        limit=20,
        name="attend",
    )(holder, lengths, queries, keep(cache_latent), keep(cache_rope))

    returned = exchange(latent_out.reshape(own * heads, KVL), ("x", "y", "z"))
    values = call(
        value_kernel,
        shape((own, heads * VH), BF16),
        [VMEM] * 3,
        name="values",
    )(regroup, returned, value_up)
    partial = call(
        output_kernel,
        shape((batch, out_proj.shape[1]), BF16),
        [VMEM] * 4,
        name="output",
    )(order, values, swap_cores(values), out_proj)
    partial = exchange(partial, ("x", "y"))
    partial = partial.reshape(groups, batch // groups, out_proj.shape[1])
    return jnp.sum(partial.astype(F32), axis=0).astype(BF16)


def solution(mesh):
    mesh = Mesh(mesh.devices.reshape(4, 2, 4, 4), ("z", "c", "x", "y"))
    gx, gy, both = ("z", "c"), ("x", "y"), ("z", "c", "x", "y")
    in_specs = (
        P(None, gx),
        P(gx, gy),
        P(gy, None, None),
        P(gy, None, None),
        P(gy, gx),
        P(both, None, None),
        P(both, None, None),
        P(),
        P(),
    )
    out_specs = P(gy, gx)
    return jax.shard_map(local, mesh=mesh, in_specs=in_specs, out_specs=out_specs, check_vma=False)
```
